32 devices in a mesh: grp: 1, var: 4 (over z), smp: 4 (over y, x), sub: 2 (over core).
Axes of the slice: x: 2, y: 2, z: 4, core: 2. Of those that a mesh axis runs over, the one named last changes fastest.
Arguments:
- dosages: bfloat16 [4096, 1024], P(('smp', 'sub'), ('grp', 'var')), may hold values from 0 to 2
- reach_blk: int32 [8], P('grp'), may hold values from 0 to 12, as said below
- locus_start: int32 [32], P('grp'), may hold values from 0 to 7
- locus_end: int32 [32], P('grp'), may hold values from 0 to 7, as said below
- locus_effects: bfloat16 [32, 1024], P(('grp', 'var', 'smp', 'sub')), may hold values from -6 to 6
Outputs:
- locus_scores: float32 [32, 1024], P(('grp', 'var', 'smp', 'sub'))
The draws below stay inside these ranges and needn't reach their ends.
Inputs may be any that keep to these rules, and one draw needn't show every extreme that they name: `reach_blk`: every value from 0 to 12 may occur, and 12 occurs in every draw. locus_end - locus_start + 1 lies in 1 to 8, and is 8 for some locus in every draw; loci may intersect one another.
All inputs are finite; a program needn't handle non-finite values.
Results may differ from the reference program's by a relative error of at most 0.0003.
Values may be sent and summed in bfloat16 or wider, within the bound.
A program may use at most 64 MiB of HBM per device.

```python
import jax
import jax.numpy as jnp
from jax import lax

BLK = 128
STRIPE_BLKS = 2
REACH = 12
LMAX = 8
SMP_DEV = 512
HALO = 1536
NLOC = 32
LPOS = 1024
N_VAR = 4
N_SMP = 4
N_SUB = 2


def draw_dosages(key, part):
    samples = SMP_DEV * N_SMP * N_SUB
    block_count = STRIPE_BLKS * N_VAR
    decay = jnp.exp(-1.0 / (4.0 * BLK))
    offsets = jnp.arange(BLK, dtype=jnp.float32)
    lag_mat = offsets[None, :] - offsets[:, None]
    kernel = jnp.where(lag_mat >= 0, jnp.sqrt(1.0 - decay * decay) * decay ** jnp.maximum(lag_mat, 0.0), 0.0)
    carry_gain = decay ** (offsets + 1.0)
    level = 2.0 * jnp.arange(samples, dtype=jnp.float32) / samples - 1.0
    start_state = jax.random.normal(jax.random.fold_in(key, 11), (samples,), jnp.float32)

    def one_block(state, block_index):
        subkeys = jax.random.split(jax.random.fold_in(key, 100 + block_index), 5)
        innov = jax.random.normal(subkeys[0], (samples, BLK), jnp.float32)
        rough = 0.7 * jax.random.normal(subkeys[1], (samples, BLK), jnp.float32)
        smooth = jnp.dot(innov, kernel, precision=lax.Precision.HIGHEST) + state[:, None] * carry_gain[None, :]
        loading = 0.6 * jax.random.normal(subkeys[2], (BLK,), jnp.float32)
        shift = jax.random.uniform(subkeys[3], (BLK,), jnp.float32, -1.5, 1.5)
        sharp = jax.random.uniform(subkeys[4], (BLK,), jnp.float32, 0.8, 2.0)
        latent = (smooth + rough + level[:, None] * loading[None, :]) * sharp[None, :] + shift[None, :]
        return (smooth[:, -1], 2.0 * jax.nn.sigmoid(latent))
    _, blocks = lax.scan(one_block, start_state, jnp.arange(block_count, dtype=jnp.int32))
    return jnp.transpose(blocks, (1, 0, 2)).reshape(samples, block_count * BLK).astype(jnp.bfloat16)


def draw_reach_blk(key, part):
    block_count = STRIPE_BLKS * N_VAR
    first_key, second_key = jax.random.split(jax.random.fold_in(key, 3))
    reach = jax.random.randint(first_key, (block_count,), 0, REACH + 1, dtype=jnp.int32)
    where_max = jax.random.randint(second_key, (), 0, block_count, dtype=jnp.int32)
    return reach.at[where_max].set(REACH).astype(jnp.int32)


def locus_bounds(key):
    locus_count = N_VAR * N_SMP * N_SUB
    block_count = STRIPE_BLKS * N_VAR
    subkeys = jax.random.split(jax.random.fold_in(key, 7), 3)
    lengths = jax.random.randint(subkeys[0], (locus_count,), 1, LMAX + 1, dtype=jnp.int32)
    longest = jax.random.randint(subkeys[1], (), 0, locus_count, dtype=jnp.int32)
    lengths = lengths.at[longest].set(LMAX)
    starts = jax.random.randint(subkeys[2], (locus_count,), 0, block_count - lengths + 1, dtype=jnp.int32)
    return (starts.astype(jnp.int32), (starts + lengths - 1).astype(jnp.int32))


def draw_locus_start(key, part):
    return locus_bounds(key)[0]


def draw_locus_end(key, part):
    return locus_bounds(key)[1]


def block_levels(rng, extent, cuts, smallest, top_value):
    loudness = 1.0
    for dim, shards_of in cuts:
        draws = jax.random.uniform(jax.random.fold_in(jax.random.fold_in(rng, 6), dim), (shards_of,), jnp.float32, smallest / len(cuts), top_value / len(cuts))
        loudness = loudness * jnp.repeat(jnp.exp(draws), extent[dim] // shards_of).reshape((-1,) + (1,) * (len(extent) - 1 - dim))
    return loudness


def gaussian(own_key, shape, deviation, bound, cuts=(), held_as=jnp.bfloat16):
    values = jax.random.normal(own_key, shape, jnp.float32) * deviation
    if len(cuts) > 0:
        values = block_levels(own_key, shape, cuts, -0.22, 0.18) * values
    return jnp.clip(values, min=-bound, max=bound).astype(held_as)


def setup_inputs(seed: int = 0, part: int = 0) -> dict:
    keys = jax.random.split(jax.random.key(seed), 6)
    own_keys = jax.random.split(jax.random.fold_in(keys[5], part), 6)
    return {
        "dosages": draw_dosages(jax.random.fold_in(jax.random.fold_in(keys[5], part), 71), part),
        "reach_blk": draw_reach_blk(jax.random.fold_in(jax.random.fold_in(keys[5], part), 71), part),
        "locus_start": draw_locus_start(jax.random.fold_in(jax.random.fold_in(keys[5], part), 71), part),
        "locus_end": draw_locus_end(jax.random.fold_in(jax.random.fold_in(keys[5], part), 71), part),
        "locus_effects": gaussian(own_keys[4], (NLOC, LPOS), 1.0, 6.0, ((0, 32),)),
    }


EPS = 1e-05
HIGHEST = lax.Precision.HIGHEST

def reference(dosages, reach_blk, locus_start, locus_end, locus_effects):
    samples = dosages.shape[0]
    variant_count = dosages.shape[1]
    block_count = variant_count // BLK
    win_cols = (REACH + 1) * BLK
    col_blocks = dosages.reshape(samples, block_count, BLK)

    def stats(block_index):
        column = lax.dynamic_index_in_dim(col_blocks, block_index, 1, keepdims=False).astype(jnp.float32)
        col_mean = lax.optimization_barrier(jnp.sum(column, axis=0)) / samples
        spread = lax.optimization_barrier(jnp.sum(jnp.square(column - col_mean[None, :]), axis=0))
        return (col_mean, lax.rsqrt(spread / samples + EPS))
    means, inverse = lax.map(stats, jnp.arange(block_count, dtype=jnp.int32))
    mean_all = jnp.concatenate([means.reshape(-1), jnp.zeros((HALO,), jnp.float32)])
    inv_all = jnp.concatenate([inverse.reshape(-1), jnp.ones((HALO,), jnp.float32)])
    padded = jnp.concatenate([dosages, jnp.zeros((samples, HALO), dosages.dtype)], axis=1)
    locus_count = locus_start.shape[0]
    lengths = locus_end - locus_start + 1
    slot_pos = jnp.arange(LPOS, dtype=jnp.int32)
    live_slot = slot_pos[None, :] < (lengths * BLK)[:, None]
    effects = jnp.where(live_slot, locus_effects.astype(jnp.float32), 0.0)
    total_cols = variant_count + HALO + LPOS

    def place(first, values):
        return lax.dynamic_update_slice_in_dim(jnp.zeros((total_cols,), jnp.float32), values, (first * BLK).astype(jnp.int32), 0)
    spread_eff = jax.vmap(place)(locus_start, effects)

    def step(accum, block_index):
        first = (block_index * BLK).astype(jnp.int32)
        rows_dos = lax.dynamic_slice_in_dim(dosages, first, BLK, 1)
        window = lax.dynamic_slice_in_dim(padded, first, win_cols, 1)
        cross_prod = lax.dot_general(rows_dos, window, (((0,), (0,)), ((), ())), preferred_element_type=jnp.float32)
        row_mean = lax.dynamic_slice_in_dim(mean_all, first, BLK, 0)
        row_inv = lax.dynamic_slice_in_dim(inv_all, first, BLK, 0)
        col_mean = lax.dynamic_slice_in_dim(mean_all, first, win_cols, 0)
        col_inv = lax.dynamic_slice_in_dim(inv_all, first, win_cols, 0)
        ld_corr = (cross_prod / samples - row_mean[:, None] * col_mean[None, :]) * (row_inv[:, None] * col_inv[None, :])
        block_gap = jnp.arange(win_cols, dtype=jnp.int32) // BLK
        keep_mask = (block_gap <= reach_blk[block_index]) & (block_index + block_gap < block_count)
        band_corr = jnp.where(keep_mask[None, :], ld_corr, 0.0)
        strict = jnp.where((block_gap > 0)[None, :], band_corr, 0.0)
        b_window = lax.dynamic_slice_in_dim(spread_eff, first, win_cols, 1)
        b_rows = lax.dynamic_slice_in_dim(spread_eff, first, BLK, 1)
        y_rows = jnp.dot(b_window, band_corr.T, precision=HIGHEST)
        y_cols = jnp.dot(b_rows, strict, precision=HIGHEST)
        current = lax.dynamic_slice_in_dim(accum, first, win_cols, 1)
        current = current + y_cols + jnp.pad(y_rows, ((0, 0), (0, win_cols - BLK)))
        return (lax.dynamic_update_slice_in_dim(accum, current, first, 1), None)
    accum, _ = lax.scan(step, jnp.zeros((locus_count, total_cols), jnp.float32), jnp.arange(block_count, dtype=jnp.int32))

    def pick(first, values):
        return lax.dynamic_slice_in_dim(values, (first * BLK).astype(jnp.int32), LPOS, 0)
    scores = jax.vmap(pick)(locus_start, accum)
    return jnp.where(live_slot, scores, 0.0)
```

```python
import functools

import jax
import jax.numpy as jnp
from jax import lax
from jax.experimental import pallas as pl
from jax.experimental.pallas import tpu as pltpu
from jax.sharding import PartitionSpec as P

BLK = 128
REACH = 12
LMAX = 8


EPS = 1e-05
HIGHEST = lax.Precision.HIGHEST


def shifted(block, axis, distance):
    devices = range(lax.axis_size(axis))
    route = [(i - distance, i) for i in devices if i - distance in devices]
    return lax.ppermute(block, axis, route)


def slot_table(locus_start, locus_end, first_blk, window_blocks):
    lengths = locus_end - locus_start + 1
    slot_ids = jnp.arange(LMAX, dtype=jnp.int32)
    target = locus_start[:, None] + slot_ids[None, :] - first_blk
    live_slot = slot_ids[None, :] < lengths[:, None]
    blocks = jnp.arange(window_blocks, dtype=jnp.int32)
    hits = live_slot[:, :, None] & (target[:, :, None] == blocks[None, None, :])
    return jnp.where(hits, 1.0, 0.0).astype(jnp.float32)


def fetch_ahead(dosages, halo_cols):
    stripe = dosages.shape[1]
    hops = (halo_cols + stripe - 1) // stripe
    pieces = [dosages]
    for distance in range(1, hops + 1):
        pieces.append(shifted(dosages, "var", -distance))
    joined = jnp.concatenate(pieces, axis=1)
    return joined


def wide_body(dosages, reach_blk, locus_start, locus_end, locus_effects):
    row_local, stripe = dosages.shape
    block_count = reach_blk.shape[0]
    locus_count = locus_start.shape[0]
    halo_cols = REACH * BLK
    window = fetch_ahead(dosages, halo_cols)
    win_cols = window.shape[1]
    shards = lax.axis_size(("smp", "sub"))
    samples = row_local * shards
    col_sum = lax.psum(jnp.sum(window, axis=0, dtype=jnp.float32), ("smp", "sub"))
    col_mean = col_sum / samples
    centred = jnp.sum(jnp.square(window.astype(jnp.float32) - col_mean[None, :]), axis=0)
    spread = lax.psum(centred, ("smp", "sub"))
    inv_sd = lax.rsqrt(spread / samples + EPS)
    cross_prod = lax.dot_general(
        dosages, window, (((0,), (0,)), ((), ())), preferred_element_type=jnp.float32
    )
    row_first = jnp.int32(0)
    ld_corr = (cross_prod / samples - col_mean[:stripe, None] * col_mean[None, :] / shards) * (
        inv_sd[:stripe, None] * inv_sd[None, :]
    )
    stripe_blocks = stripe // BLK
    first_blk = lax.axis_index("var") * stripe_blocks
    reach_local = lax.dynamic_slice_in_dim(reach_blk, first_blk, stripe_blocks)
    row_blocks = jnp.arange(stripe, dtype=jnp.int32) // BLK
    stripe_ids = jnp.arange(stripe_blocks, dtype=jnp.int32)
    reach_rows = jnp.sum(
        jnp.where(row_blocks[:, None] == stripe_ids[None, :], reach_local[None, :], 0), axis=1
    )
    col_blocks = jnp.arange(win_cols, dtype=jnp.int32) // BLK
    block_gap = col_blocks[None, :] - row_blocks[:, None]
    keep_mask = (
        (block_gap >= 0)
        & (block_gap <= reach_rows[:, None])
        & (first_blk + col_blocks[None, :] < block_count)
    )
    band_corr = jnp.where(keep_mask, ld_corr, 0.0)
    strict = jnp.where(block_gap > 0, band_corr, 0.0)
    window_blocks = win_cols // BLK
    lookup = slot_table(locus_start, locus_end, first_blk, window_blocks)
    gathered = lax.all_gather(locus_effects, ("var", "smp", "sub"), axis=0, tiled=True)
    effects = gathered.astype(jnp.float32).reshape(locus_count, LMAX, BLK)
    b_window = jnp.einsum("lkw,lkc->lwc", lookup, effects, precision=HIGHEST).reshape(
        locus_count, win_cols
    )
    b_rows = lax.dynamic_slice_in_dim(b_window, row_first, stripe, 1)
    y_rows = jnp.dot(b_window, band_corr.T, precision=HIGHEST)
    y_cols = jnp.dot(b_rows, strict, precision=HIGHEST)
    y_window = y_cols + lax.dynamic_update_slice_in_dim(
        jnp.zeros_like(y_cols), y_rows, row_first, 1
    )
    scores = jnp.einsum(
        "lkw,lwc->lkc", lookup, y_window.reshape(locus_count, window_blocks, BLK), precision=HIGHEST
    )
    return lax.psum_scatter(
        scores.reshape(locus_count, LMAX * BLK),
        ("var", "smp", "sub"),
        scatter_dimension=0,
        tiled=True,
    )


MESH = pl.DeviceIdType.MESH


def halves(values):
    high = values.astype(jnp.bfloat16)
    low = (values - high.astype(jnp.float32)).astype(jnp.bfloat16)
    return jnp.concatenate([high, low], axis=0)


def kernel(n_var, n_smp, n_sub, dos_any, reach, start, end, eff_ref, out_ref,
           local, x, st, ms, e, y, ry, rs, rz,
           local_sem, x_s, x_r, st_s, st_r, ms_s, ms_r, e1_s, e1_r, e2_s, e2_r,
           ry_s, ry_r, rz_s, rz_r):
    n_pl = n_smp * n_sub
    rows, stripe = dos_any.shape
    part = rows // n_var
    per_stripe = stripe // BLK
    blocks = n_var * per_stripe
    loci = n_var * n_pl
    samples = rows * n_pl
    v = lax.axis_index("var")
    p = lax.axis_index("smp") * n_sub + lax.axis_index("sub")

    def var_peer(d):
        t = lax.rem(v + d, n_var)
        return t, {"var": t}

    def plane_peer(d):
        q = lax.rem(p + d, n_pl)
        return q, {"smp": lax.div(q, n_sub), "sub": lax.rem(q, n_sub)}

    def rows_of(index, count):
        return pl.ds(pl.multiple_of(index * count, count), count)

    def send(src, dst, s_sem, r_sem, peer):
        copy = pltpu.make_async_remote_copy(
            src_ref=src, dst_ref=dst, send_sem=s_sem, recv_sem=r_sem,
            device_id=peer, device_id_type=MESH)
        copy.start()
        return copy

    whole = pltpu.make_async_copy(dos_any, local, local_sem.at[0])
    whole.start()
    own = pltpu.make_async_copy(dos_any.at[rows_of(v, part), :], x.at[v], local_sem.at[1])
    own.start()

    barrier = pltpu.get_barrier_semaphore()
    for d in range(1, n_var):
        pl.semaphore_signal(barrier, inc=1, device_id=var_peer(d)[1], device_id_type=MESH)
    for d in range(1, n_pl):
        pl.semaphore_signal(barrier, inc=1, device_id=plane_peer(d)[1], device_id_type=MESH)

    me = v * n_pl + p
    first, last = start[me], end[me]
    block_row = lax.broadcasted_iota(jnp.int32, (blocks, BLK), 0)
    eff = eff_ref[...].astype(jnp.float32)
    placed = jnp.zeros((blocks, BLK), jnp.float32)
    for k in range(eff.shape[1] // BLK):
        hit = (block_row == first + k) & (block_row <= last)
        placed = placed + jnp.where(hit, eff[:, k * BLK:(k + 1) * BLK], 0.0)
    own_rows = rows_of(p * n_var + v, blocks)
    e[own_rows, :] = placed

    pl.semaphore_wait(barrier, n_var - 1 + n_pl - 1)
    e1 = [send(e.at[own_rows, :], e.at[own_rows, :], e1_s.at[d], e1_r.at[d], var_peer(d)[1])
          for d in range(1, n_var)]
    xs = []
    for d in range(1, n_var):
        t, peer = var_peer(d)
        xs.append(send(dos_any.at[rows_of(t, part), :], x.at[v], x_s.at[d], x_r.at[d], peer))

    whole.wait()
    mine = local[...].astype(jnp.float32)
    total = jnp.sum(mine, axis=0, keepdims=True)
    sq = jnp.sum(jnp.square(mine - total / rows), axis=0, keepdims=True)
    st[p, 0:1, :] = total
    st[p, 1:2, :] = sq
    sts = [send(st.at[p], st.at[p], st_s.at[d], st_r.at[d], plane_peer(d)[1])
           for d in range(1, n_pl)]

    for copy in e1:
        copy.wait()
    group = rows_of(p, n_var * blocks)
    e2 = [send(e.at[group, :], e.at[group, :], e2_s.at[d], e2_r.at[d], plane_peer(d)[1])
          for d in range(1, n_pl)]

    for copy in sts:
        copy.wait()
    mean = st[0, 0:1, :]
    for q in range(1, n_pl):
        mean = mean + st[q, 0:1, :]
    mean = mean / samples
    spread = jnp.zeros_like(mean)
    for q in range(n_pl):
        spread = spread + (st[q, 1:2, :] + rows * jnp.square(st[q, 0:1, :] / rows - mean))
    ms[v, 0:1, :] = mean
    ms[v, 1:2, :] = lax.rsqrt(spread / samples + EPS)
    mss = [send(ms.at[v], ms.at[v], ms_s.at[d], ms_r.at[d], var_peer(d)[1])
           for d in range(1, n_var)]
    for copy in e2:
        copy.wait()
    for copy in mss:
        copy.wait()
    own.wait()
    for copy in xs:
        copy.wait()

    def cols(j):
        return j // per_stripe, slice((j % per_stripe) * BLK, (j % per_stripe + 1) * BLK)

    parts = []
    for j in range(blocks):
        s, c = cols(j)
        z = e[pl.ds(j, loci, stride=blocks), :] * ms[s, 1:2, c]
        w = lax.dot_general(halves(z), x[s, :, c], (((1,), (1,)), ((), ())),
                            preferred_element_type=jnp.float32)
        shift = jnp.sum(z * ms[s, 0:1, c], axis=1, keepdims=True)
        parts.append(w[:loci] + w[loci:] - shift)
    for i in range(blocks):
        s, c = cols(i)
        summed = parts[i]
        for j in range(blocks):
            if j != i:
                low, high = min(i, j), max(i, j)
                summed = summed + jnp.where(reach[low] >= high - low, 1.0, 0.0) * parts[j]
        r = lax.dot_general(halves(summed), x[s, :, c], (((1,), (0,)), ((), ())),
                            preferred_element_type=jnp.float32)
        y[pl.ds(i, loci, stride=blocks), :] = (r[:loci] + r[loci:]) * (ms[s, 1:2, c] / samples)

    rys = []
    for d in range(1, n_pl):
        q, peer = plane_peer(d)
        rys.append(send(y.at[rows_of(q, n_var * blocks), :], ry.at[p], ry_s.at[d], ry_r.at[d], peer))
    ry[p] = y[group, :]
    for copy in rys:
        copy.wait()
    acc = ry[0]
    for q in range(1, n_pl):
        acc = acc + ry[q]
    rs[...] = acc
    rzs = []
    for d in range(1, n_var):
        t, peer = var_peer(d)
        rzs.append(send(rs.at[rows_of(t, blocks), :], rz.at[v], rz_s.at[d], rz_r.at[d], peer))
    rz[v] = rs[rows_of(v, blocks), :]
    for copy in rzs:
        copy.wait()
    score = rz[0]
    for t in range(1, n_var):
        score = score + rz[t]
    for k in range(eff.shape[1] // BLK):
        hit = (block_row == first + k) & (block_row <= last)
        out_ref[:, k * BLK:(k + 1) * BLK] = jnp.sum(jnp.where(hit, score, 0.0), axis=0, keepdims=True)


def slab_body(dosages, reach_blk, locus_start, locus_end, locus_effects):
    n_var, n_smp, n_sub = (lax.axis_size(a) for a in ("var", "smp", "sub"))
    n_pl = n_smp * n_sub
    rows, stripe = dosages.shape
    blocks = reach_blk.shape[0]
    loci = locus_start.shape[0]
    f32 = jnp.float32
    dma = pltpu.SemaphoreType.DMA
    smem = pl.BlockSpec(memory_space=pltpu.SMEM)
    vmem = pl.BlockSpec(memory_space=pltpu.VMEM)
    return pl.pallas_call(
        functools.partial(kernel, n_var, n_smp, n_sub),
        out_shape=jax.ShapeDtypeStruct(locus_effects.shape, f32),
        in_specs=[pl.BlockSpec(memory_space=pl.ANY), smem, smem, smem, vmem],
        out_specs=vmem,
        scratch_shapes=[
            pltpu.VMEM((rows, stripe), dosages.dtype),
            pltpu.VMEM((n_var, rows // n_var, stripe), dosages.dtype),
            pltpu.VMEM((n_pl, 2, stripe), f32),
            pltpu.VMEM((n_var, 2, stripe), f32),
            pltpu.VMEM((loci * blocks, BLK), f32),
            pltpu.VMEM((loci * blocks, BLK), f32),
            pltpu.VMEM((n_pl, n_var * blocks, BLK), f32),
            pltpu.VMEM((n_var * blocks, BLK), f32),
            pltpu.VMEM((n_var, blocks, BLK), f32),
            dma((2,)),
            dma((n_var,)), dma((n_var,)),
            dma((n_pl,)), dma((n_pl,)),
            dma((n_var,)), dma((n_var,)),
            dma((n_var,)), dma((n_var,)),
            dma((n_pl,)), dma((n_pl,)),
            dma((n_pl,)), dma((n_pl,)),
            dma((n_var,)), dma((n_var,)),
        ],
        compiler_params=pltpu.CompilerParams(
            collective_id=0, has_side_effects=True, vmem_limit_bytes=16 * 1024 * 1024),
    )(dosages, reach_blk, locus_start, locus_end, locus_effects)


def body(dosages, reach_blk, locus_start, locus_end, locus_effects):
    blocks = reach_blk.shape[0]
    devices = lax.axis_size(("var", "smp", "sub"))
    short = blocks * BLK == locus_effects.shape[1] and locus_start.shape[0] == devices
    run = slab_body if short else wide_body
    return run(dosages, reach_blk, locus_start, locus_end, locus_effects)


def solution(mesh):
    in_specs = (
        P(("smp", "sub"), ("grp", "var")),
        P("grp"),
        P("grp"),
        P("grp"),
        P(("grp", "var", "smp", "sub"), None),
    )
    out_specs = P(("grp", "var", "smp", "sub"), None)
    return jax.shard_map(body, mesh=mesh, in_specs=in_specs, out_specs=out_specs, check_vma=False)
```

```python
import functools

import jax
import jax.numpy as jnp
from jax import lax
from jax.experimental import pallas as pl
from jax.experimental.pallas import tpu as pltpu
from jax.sharding import PartitionSpec as P

BLK = 128
REACH = 12
LMAX = 8


EPS = 1e-05
HIGHEST = lax.Precision.HIGHEST


def shifted(block, axis, distance):
    devices = range(lax.axis_size(axis))
    route = [(i - distance, i) for i in devices if i - distance in devices]
    return lax.ppermute(block, axis, route)


def slot_table(locus_start, locus_end, first_blk, window_blocks):
    lengths = locus_end - locus_start + 1
    slot_ids = jnp.arange(LMAX, dtype=jnp.int32)
    target = locus_start[:, None] + slot_ids[None, :] - first_blk
    live_slot = slot_ids[None, :] < lengths[:, None]
    blocks = jnp.arange(window_blocks, dtype=jnp.int32)
    hits = live_slot[:, :, None] & (target[:, :, None] == blocks[None, None, :])
    return jnp.where(hits, 1.0, 0.0).astype(jnp.float32)


def fetch_ahead(dosages, halo_cols):
    stripe = dosages.shape[1]
    hops = (halo_cols + stripe - 1) // stripe
    pieces = [dosages]
    for distance in range(1, hops + 1):
        pieces.append(shifted(dosages, "var", -distance))
    joined = jnp.concatenate(pieces, axis=1)
    return joined


def wide_body(dosages, reach_blk, locus_start, locus_end, locus_effects):
    row_local, stripe = dosages.shape
    block_count = reach_blk.shape[0]
    locus_count = locus_start.shape[0]
    halo_cols = REACH * BLK
    window = fetch_ahead(dosages, halo_cols)
    win_cols = window.shape[1]
    shards = lax.axis_size(("smp", "sub"))
    samples = row_local * shards
    col_sum = lax.psum(jnp.sum(window, axis=0, dtype=jnp.float32), ("smp", "sub"))
    col_mean = col_sum / samples
    centred = jnp.sum(jnp.square(window.astype(jnp.float32) - col_mean[None, :]), axis=0)
    spread = lax.psum(centred, ("smp", "sub"))
    inv_sd = lax.rsqrt(spread / samples + EPS)
    cross_prod = lax.dot_general(
        dosages, window, (((0,), (0,)), ((), ())), preferred_element_type=jnp.float32
    )
    row_first = jnp.int32(0)
    ld_corr = (cross_prod / samples - col_mean[:stripe, None] * col_mean[None, :] / shards) * (
        inv_sd[:stripe, None] * inv_sd[None, :]
    )
    stripe_blocks = stripe // BLK
    first_blk = lax.axis_index("var") * stripe_blocks
    reach_local = lax.dynamic_slice_in_dim(reach_blk, first_blk, stripe_blocks)
    row_blocks = jnp.arange(stripe, dtype=jnp.int32) // BLK
    stripe_ids = jnp.arange(stripe_blocks, dtype=jnp.int32)
    reach_rows = jnp.sum(
        jnp.where(row_blocks[:, None] == stripe_ids[None, :], reach_local[None, :], 0), axis=1
    )
    col_blocks = jnp.arange(win_cols, dtype=jnp.int32) // BLK
    block_gap = col_blocks[None, :] - row_blocks[:, None]
    keep_mask = (
        (block_gap >= 0)
        & (block_gap <= reach_rows[:, None])
        & (first_blk + col_blocks[None, :] < block_count)
    )
    band_corr = jnp.where(keep_mask, ld_corr, 0.0)
    strict = jnp.where(block_gap > 0, band_corr, 0.0)
    window_blocks = win_cols // BLK
    lookup = slot_table(locus_start, locus_end, first_blk, window_blocks)
    gathered = lax.all_gather(locus_effects, ("var", "smp", "sub"), axis=0, tiled=True)
    effects = gathered.astype(jnp.float32).reshape(locus_count, LMAX, BLK)
    b_window = jnp.einsum("lkw,lkc->lwc", lookup, effects, precision=HIGHEST).reshape(
        locus_count, win_cols
    )
    b_rows = lax.dynamic_slice_in_dim(b_window, row_first, stripe, 1)
    y_rows = jnp.dot(b_window, band_corr.T, precision=HIGHEST)
    y_cols = jnp.dot(b_rows, strict, precision=HIGHEST)
    y_window = y_cols + lax.dynamic_update_slice_in_dim(
        jnp.zeros_like(y_cols), y_rows, row_first, 1
    )
    scores = jnp.einsum(
        "lkw,lwc->lkc", lookup, y_window.reshape(locus_count, window_blocks, BLK), precision=HIGHEST
    )
    return lax.psum_scatter(
        scores.reshape(locus_count, LMAX * BLK),
        ("var", "smp", "sub"),
        scatter_dimension=0,
        tiled=True,
    )


MESH = pl.DeviceIdType.MESH


def halves(values):
    high = values.astype(jnp.bfloat16)
    low = (values - high.astype(jnp.float32)).astype(jnp.bfloat16)
    return jnp.concatenate([high, low], axis=0)


def kernel(n_var, n_smp, n_sub, dos_any, reach_any, start_any, end_any, eff_any, out_ref,
           reach, start, end, eff_ref, local, x, st, ms, e, y, ry,
           small_sem, local_sem, x_s, x_r, st_s, st_r, ms_s, ms_r, e1_s, e1_r, e2_s, e2_r,
           ry_s, ry_r):
    n_pl = n_smp * n_sub
    rows, stripe = dos_any.shape
    part = rows // n_var
    per_stripe = stripe // BLK
    blocks = n_var * per_stripe
    loci = n_var * n_pl
    samples = rows * n_pl
    v = lax.axis_index("var")
    p = lax.axis_index("smp") * n_sub + lax.axis_index("sub")

    def var_peer(d):
        t = lax.rem(v + d, n_var)
        return t, {"var": t}

    def plane_peer(d):
        q = lax.rem(p + d, n_pl)
        return q, {"smp": lax.div(q, n_sub), "sub": lax.rem(q, n_sub)}

    def any_peer(d):
        g = lax.rem(p * n_var + v + d, loci)
        q = lax.div(g, n_var)
        return g, {"var": lax.rem(g, n_var), "smp": lax.div(q, n_sub), "sub": lax.rem(q, n_sub)}

    def rows_of(index, count):
        return pl.ds(pl.multiple_of(index * count, count), count)

    def send(src, dst, s_sem, r_sem, peer):
        copy = pltpu.make_async_remote_copy(
            src_ref=src, dst_ref=dst, send_sem=s_sem, recv_sem=r_sem,
            device_id=peer, device_id_type=MESH)
        copy.start()
        return copy

    small = [pltpu.make_async_copy(src, dst, small_sem.at[n]) for n, (src, dst) in enumerate((
        (eff_any, eff_ref), (start_any, start), (end_any, end), (reach_any, reach)))]
    for copy in small:
        copy.start()
    whole = pltpu.make_async_copy(dos_any, local, local_sem.at[0])
    whole.start()
    own = pltpu.make_async_copy(dos_any.at[rows_of(v, part), :], x.at[v], local_sem.at[1])
    own.start()

    barrier = pltpu.get_barrier_semaphore()
    for d in range(1, loci):
        pl.semaphore_signal(barrier, inc=1, device_id=any_peer(d)[1], device_id_type=MESH)

    for copy in small:
        copy.wait()
    me = v * n_pl + p
    first, last = start[me], end[me]
    block_row = lax.broadcasted_iota(jnp.int32, (blocks, BLK), 0)
    eff = eff_ref[...].astype(jnp.float32)
    placed = jnp.zeros((blocks, BLK), jnp.float32)
    for k in range(eff.shape[1] // BLK):
        hit = (block_row == first + k) & (block_row <= last)
        placed = placed + jnp.where(hit, eff[:, k * BLK:(k + 1) * BLK], 0.0)
    own_rows = rows_of(p * n_var + v, blocks)
    e[own_rows, :] = placed

    pl.semaphore_wait(barrier, loci - 1)
    e1 = [send(e.at[own_rows, :], e.at[own_rows, :], e1_s.at[d], e1_r.at[d], var_peer(d)[1])
          for d in range(1, n_var)]
    xs = []
    for d in range(1, n_var):
        t, peer = var_peer(d)
        xs.append(send(dos_any.at[rows_of(t, part), :], x.at[v], x_s.at[d], x_r.at[d], peer))

    whole.wait()
    mine = local[...].astype(jnp.float32)
    total = jnp.sum(mine, axis=0, keepdims=True)
    sq = jnp.sum(jnp.square(mine - total / rows), axis=0, keepdims=True)
    st[p, 0:1, :] = total
    st[p, 1:2, :] = sq
    sts = [send(st.at[p], st.at[p], st_s.at[d], st_r.at[d], plane_peer(d)[1])
           for d in range(1, n_pl)]

    for copy in e1:
        copy.wait()
    group = rows_of(p, n_var * blocks)
    e2 = [send(e.at[group, :], e.at[group, :], e2_s.at[d], e2_r.at[d], plane_peer(d)[1])
          for d in range(1, n_pl)]

    for copy in sts:
        copy.wait()
    mean = st[0, 0:1, :]
    for q in range(1, n_pl):
        mean = mean + st[q, 0:1, :]
    mean = mean / samples
    spread = jnp.zeros_like(mean)
    for q in range(n_pl):
        spread = spread + (st[q, 1:2, :] + rows * jnp.square(st[q, 0:1, :] / rows - mean))
    ms[v, 0:1, :] = mean
    var_eps = spread / samples + EPS
    inv = lax.rsqrt(var_eps)
    ms[v, 1:2, :] = inv * (1.5 - 0.5 * var_eps * inv * inv)
    mss = [send(ms.at[v], ms.at[v], ms_s.at[d], ms_r.at[d], var_peer(d)[1])
           for d in range(1, n_var)]
    for copy in e2:
        copy.wait()
    for copy in mss:
        copy.wait()
    own.wait()
    for copy in xs:
        copy.wait()

    def cols(j):
        return j // per_stripe, slice((j % per_stripe) * BLK, (j % per_stripe + 1) * BLK)

    parts = []
    for j in range(blocks):
        s, c = cols(j)
        z = e[pl.ds(j, loci, stride=blocks), :] * ms[s, 1:2, c]
        w = lax.dot_general(halves(z), x[s, :, c], (((1,), (1,)), ((), ())),
                            preferred_element_type=jnp.float32)
        shift = jnp.sum(z * ms[s, 0:1, c], axis=1, keepdims=True)
        parts.append(w[:loci] + w[loci:] - shift)
    for i in range(blocks):
        s, c = cols(i)
        summed = parts[i]
        for j in range(blocks):
            if j != i:
                low, high = min(i, j), max(i, j)
                summed = summed + jnp.where(reach[low] >= high - low, 1.0, 0.0) * parts[j]
        r = lax.dot_general(halves(summed), x[s, :, c], (((1,), (0,)), ((), ())),
                            preferred_element_type=jnp.float32)
        y[pl.ds(i, loci, stride=blocks), :] = (r[:loci] + r[loci:]) * (ms[s, 1:2, c] / samples)

    for d in range(1, loci):
        g, peer = any_peer(d)
        send(y.at[rows_of(g, blocks), :], ry.at[d], ry_s.at[0], ry_r.at[0], peer)
    score = y[own_rows, :]
    sent = y.at[pl.ds(0, (loci - 1) * blocks), :]
    landed = ry.at[pl.ds(1, loci - 1)]
    pltpu.make_async_copy(sent, sent, ry_s.at[0]).wait()
    pltpu.make_async_copy(landed, landed, ry_r.at[0]).wait()
    for d in range(1, loci):
        score = score + ry[d]
    for k in range(eff.shape[1] // BLK):
        hit = (block_row == first + k) & (block_row <= last)
        out_ref[:, k * BLK:(k + 1) * BLK] = jnp.sum(jnp.where(hit, score, 0.0), axis=0, keepdims=True)


def slab_body(dosages, reach_blk, locus_start, locus_end, locus_effects):
    n_var, n_smp, n_sub = (lax.axis_size(a) for a in ("var", "smp", "sub"))
    n_pl = n_smp * n_sub
    rows, stripe = dosages.shape
    blocks = reach_blk.shape[0]
    loci = locus_start.shape[0]
    f32 = jnp.float32
    dma = pltpu.SemaphoreType.DMA
    hbm = pl.BlockSpec(memory_space=pltpu.HBM)
    vmem = pl.BlockSpec(memory_space=pltpu.VMEM)
    return pl.pallas_call(
        functools.partial(kernel, n_var, n_smp, n_sub),
        out_shape=jax.ShapeDtypeStruct(locus_effects.shape, f32),
        in_specs=[hbm] * 5,
        out_specs=vmem,
        scratch_shapes=[
            pltpu.SMEM(reach_blk.shape, reach_blk.dtype),
            pltpu.SMEM(locus_start.shape, locus_start.dtype),
            pltpu.SMEM(locus_end.shape, locus_end.dtype),
            pltpu.VMEM(locus_effects.shape, locus_effects.dtype),
            pltpu.VMEM((rows, stripe), dosages.dtype),
            pltpu.VMEM((n_var, rows // n_var, stripe), dosages.dtype),
            pltpu.VMEM((n_pl, 2, stripe), f32),
            pltpu.VMEM((n_var, 2, stripe), f32),
            pltpu.VMEM((loci * blocks, BLK), f32),
            pltpu.VMEM((loci * blocks, BLK), f32),
            pltpu.VMEM((loci, blocks, BLK), f32),
            dma((4,)), dma((2,)),
            dma((n_var,)), dma((n_var,)),
            dma((n_pl,)), dma((n_pl,)),
            dma((n_var,)), dma((n_var,)),
            dma((n_var,)), dma((n_var,)),
            dma((n_pl,)), dma((n_pl,)),
            dma((1,)), dma((1,)),
        ],
        compiler_params=pltpu.CompilerParams(
            collective_id=0, has_side_effects=True, vmem_limit_bytes=60 * 1024 * 1024),
    )(dosages, reach_blk, locus_start, locus_end, locus_effects)


def body(dosages, reach_blk, locus_start, locus_end, locus_effects):
    blocks = reach_blk.shape[0]
    devices = lax.axis_size(("var", "smp", "sub"))
    short = blocks * BLK == locus_effects.shape[1] and locus_start.shape[0] == devices
    run = slab_body if short else wide_body
    return run(dosages, reach_blk, locus_start, locus_end, locus_effects)


def solution(mesh):
    in_specs = (
        P(("smp", "sub"), ("grp", "var")),
        P("grp"),
        P("grp"),
        P("grp"),
        P(("grp", "var", "smp", "sub"), None),
    )
    out_specs = P(("grp", "var", "smp", "sub"), None)
    return jax.shard_map(body, mesh=mesh, in_specs=in_specs, out_specs=out_specs, check_vma=False)
```

```python
import functools

import jax
import jax.numpy as jnp
from jax import lax
from jax.experimental import pallas as pl
from jax.experimental.pallas import tpu as pltpu
from jax.sharding import PartitionSpec as P

BLK = 128
REACH = 12
LMAX = 8


EPS = 1e-05
HIGHEST = lax.Precision.HIGHEST


def shifted(block, axis, distance):
    devices = range(lax.axis_size(axis))
    route = [(i - distance, i) for i in devices if i - distance in devices]
    return lax.ppermute(block, axis, route)


def slot_table(locus_start, locus_end, first_blk, window_blocks):
    lengths = locus_end - locus_start + 1
    slot_ids = jnp.arange(LMAX, dtype=jnp.int32)
    target = locus_start[:, None] + slot_ids[None, :] - first_blk
    live_slot = slot_ids[None, :] < lengths[:, None]
    blocks = jnp.arange(window_blocks, dtype=jnp.int32)
    hits = live_slot[:, :, None] & (target[:, :, None] == blocks[None, None, :])
    return jnp.where(hits, 1.0, 0.0).astype(jnp.float32)


def fetch_ahead(dosages, halo_cols):
    stripe = dosages.shape[1]
    hops = (halo_cols + stripe - 1) // stripe
    pieces = [dosages]
    for distance in range(1, hops + 1):
        pieces.append(shifted(dosages, "var", -distance))
    joined = jnp.concatenate(pieces, axis=1)
    return joined


def wide_body(dosages, reach_blk, locus_start, locus_end, locus_effects):
    row_local, stripe = dosages.shape
    block_count = reach_blk.shape[0]
    locus_count = locus_start.shape[0]
    halo_cols = REACH * BLK
    window = fetch_ahead(dosages, halo_cols)
    win_cols = window.shape[1]
    shards = lax.axis_size(("smp", "sub"))
    samples = row_local * shards
    col_sum = lax.psum(jnp.sum(window, axis=0, dtype=jnp.float32), ("smp", "sub"))
    col_mean = col_sum / samples
    centred = jnp.sum(jnp.square(window.astype(jnp.float32) - col_mean[None, :]), axis=0)
    spread = lax.psum(centred, ("smp", "sub"))
    inv_sd = lax.rsqrt(spread / samples + EPS)
    cross_prod = lax.dot_general(
        dosages, window, (((0,), (0,)), ((), ())), preferred_element_type=jnp.float32
    )
    row_first = jnp.int32(0)
    ld_corr = (cross_prod / samples - col_mean[:stripe, None] * col_mean[None, :] / shards) * (
        inv_sd[:stripe, None] * inv_sd[None, :]
    )
    stripe_blocks = stripe // BLK
    first_blk = lax.axis_index("var") * stripe_blocks
    reach_local = lax.dynamic_slice_in_dim(reach_blk, first_blk, stripe_blocks)
    row_blocks = jnp.arange(stripe, dtype=jnp.int32) // BLK
    stripe_ids = jnp.arange(stripe_blocks, dtype=jnp.int32)
    reach_rows = jnp.sum(
        jnp.where(row_blocks[:, None] == stripe_ids[None, :], reach_local[None, :], 0), axis=1
    )
    col_blocks = jnp.arange(win_cols, dtype=jnp.int32) // BLK
    block_gap = col_blocks[None, :] - row_blocks[:, None]
    keep_mask = (
        (block_gap >= 0)
        & (block_gap <= reach_rows[:, None])
        & (first_blk + col_blocks[None, :] < block_count)
    )
    band_corr = jnp.where(keep_mask, ld_corr, 0.0)
    strict = jnp.where(block_gap > 0, band_corr, 0.0)
    window_blocks = win_cols // BLK
    lookup = slot_table(locus_start, locus_end, first_blk, window_blocks)
    gathered = lax.all_gather(locus_effects, ("var", "smp", "sub"), axis=0, tiled=True)
    effects = gathered.astype(jnp.float32).reshape(locus_count, LMAX, BLK)
    b_window = jnp.einsum("lkw,lkc->lwc", lookup, effects, precision=HIGHEST).reshape(
        locus_count, win_cols
    )
    b_rows = lax.dynamic_slice_in_dim(b_window, row_first, stripe, 1)
    y_rows = jnp.dot(b_window, band_corr.T, precision=HIGHEST)
    y_cols = jnp.dot(b_rows, strict, precision=HIGHEST)
    y_window = y_cols + lax.dynamic_update_slice_in_dim(
        jnp.zeros_like(y_cols), y_rows, row_first, 1
    )
    scores = jnp.einsum(
        "lkw,lwc->lkc", lookup, y_window.reshape(locus_count, window_blocks, BLK), precision=HIGHEST
    )
    return lax.psum_scatter(
        scores.reshape(locus_count, LMAX * BLK),
        ("var", "smp", "sub"),
        scatter_dimension=0,
        tiled=True,
    )


MESH = pl.DeviceIdType.MESH


def halves(values):
    high = values.astype(jnp.bfloat16)
    low = (values - high.astype(jnp.float32)).astype(jnp.bfloat16)
    return jnp.concatenate([high, low], axis=0)


def rejoined(pair):
    half = pair.shape[0] // 2
    return pair[:half].astype(jnp.float32) + pair[half:].astype(jnp.float32)


def kernel(n_var, n_smp, n_sub, dos_any, reach_any, start_any, end_any, eff_any, out_ref,
           reach, start, end, eff_ref, local, x, st, ms, e, y, ry,
           small_sem, local_sem, x_s, x_r, st_s, st_r, ms_s, ms_r, e1_s, e1_r, e2_s, e2_r,
           ry_s, ry_r):
    n_pl = n_smp * n_sub
    rows, stripe = dos_any.shape
    part = rows // n_var
    per_stripe = stripe // BLK
    blocks = n_var * per_stripe
    loci = n_var * n_pl
    samples = rows * n_pl
    v = lax.axis_index("var")
    p = lax.axis_index("smp") * n_sub + lax.axis_index("sub")

    def var_peer(d):
        t = lax.rem(v + d, n_var)
        return t, {"var": t}

    def plane_peer(d):
        q = lax.rem(p + d, n_pl)
        return q, {"smp": lax.div(q, n_sub), "sub": lax.rem(q, n_sub)}

    def any_peer(d):
        g = lax.rem(p * n_var + v + d, loci)
        q = lax.div(g, n_var)
        return g, {"var": lax.rem(g, n_var), "smp": lax.div(q, n_sub), "sub": lax.rem(q, n_sub)}

    def rows_of(index, count):
        return pl.ds(pl.multiple_of(index * count, count), count)

    def send(src, dst, s_sem, r_sem, peer):
        copy = pltpu.make_async_remote_copy(
            src_ref=src, dst_ref=dst, send_sem=s_sem, recv_sem=r_sem,
            device_id=peer, device_id_type=MESH)
        copy.start()
        return copy

    barrier = pltpu.get_barrier_semaphore()
    for d in range(1, loci):
        pl.semaphore_signal(barrier, inc=1, device_id=any_peer(d)[1], device_id_type=MESH)

    small = [pltpu.make_async_copy(src, dst, small_sem.at[n]) for n, (src, dst) in enumerate((
        (eff_any, eff_ref), (start_any, start), (end_any, end), (reach_any, reach)))]
    for copy in small:
        copy.start()
    whole = pltpu.make_async_copy(dos_any, local, local_sem.at[0])
    whole.start()
    own = pltpu.make_async_copy(dos_any.at[rows_of(v, part), :], x.at[v], local_sem.at[1])
    own.start()

    for copy in small:
        copy.wait()
    me = v * n_pl + p
    first, last = start[me], end[me]
    block_row = lax.broadcasted_iota(jnp.int32, (blocks, BLK), 0)
    eff = eff_ref[...].astype(jnp.float32)
    placed = jnp.zeros((blocks, BLK), jnp.float32)
    for k in range(eff.shape[1] // BLK):
        hit = (block_row == first + k) & (block_row <= last)
        placed = placed + jnp.where(hit, eff[:, k * BLK:(k + 1) * BLK], 0.0)
    own_rows = rows_of(p * n_var + v, blocks)
    e[own_rows, :] = placed

    whole.wait()
    mine = local[...].astype(jnp.float32)
    total = jnp.sum(mine, axis=0, keepdims=True)
    sq = jnp.sum(jnp.square(mine - total / rows), axis=0, keepdims=True)
    st[p, 0:1, :] = total
    st[p, 1:2, :] = sq
    pl.semaphore_wait(barrier, loci - 1)
    e1 = [send(e.at[own_rows, :], e.at[own_rows, :], e1_s.at[d], e1_r.at[d], var_peer(d)[1])
          for d in range(1, n_var)]
    sts = [send(st.at[p], st.at[p], st_s.at[d], st_r.at[d], plane_peer(d)[1])
           for d in range(1, n_pl)]
    xs = []
    for d in range(1, n_var):
        t, peer = var_peer(d)
        xs.append(send(dos_any.at[rows_of(t, part), :], x.at[v], x_s.at[d], x_r.at[d], peer))

    for copy in e1:
        copy.wait()
    group = rows_of(p, n_var * blocks)
    e2 = [send(e.at[group, :], e.at[group, :], e2_s.at[d], e2_r.at[d], plane_peer(d)[1])
          for d in range(1, n_pl)]

    for copy in sts:
        copy.wait()
    mean = st[0, 0:1, :]
    for q in range(1, n_pl):
        mean = mean + st[q, 0:1, :]
    mean = mean / samples
    spread = jnp.zeros_like(mean)
    for q in range(n_pl):
        spread = spread + (st[q, 1:2, :] + rows * jnp.square(st[q, 0:1, :] / rows - mean))
    ms[v, 0:1, :] = mean
    var_eps = spread / samples + EPS
    inv = lax.rsqrt(var_eps)
    ms[v, 1:2, :] = inv * (1.5 - 0.5 * var_eps * inv * inv)
    mss = [send(ms.at[v], ms.at[v], ms_s.at[d], ms_r.at[d], var_peer(d)[1])
           for d in range(1, n_var)]
    for copy in e2:
        copy.wait()
    for copy in mss:
        copy.wait()
    own.wait()
    for copy in xs:
        copy.wait()

    def cols(j):
        return j // per_stripe, slice((j % per_stripe) * BLK, (j % per_stripe + 1) * BLK)

    parts = []
    for j in range(blocks):
        s, c = cols(j)
        z = e[pl.ds(j, loci, stride=blocks), :] * ms[s, 1:2, c]
        pair = halves(z)
        w = lax.dot_general(pair, x[s, :, c], (((1,), (1,)), ((), ())),
                            preferred_element_type=jnp.float32)
        shift = jnp.sum(rejoined(pair) * ms[s, 0:1, c], axis=1, keepdims=True)
        parts.append(w[:loci] + w[loci:] - shift)
    for i in range(blocks):
        s, c = cols(i)
        summed = parts[i]
        for j in range(blocks):
            if j != i:
                low, high = min(i, j), max(i, j)
                summed = summed + jnp.where(reach[low] >= high - low, 1.0, 0.0) * parts[j]
        r = lax.dot_general(halves(summed), x[s, :, c], (((1,), (0,)), ((), ())),
                            preferred_element_type=jnp.float32)
        y[pl.ds(i, loci, stride=blocks), :] = (r[:loci] + r[loci:]) * (ms[s, 1:2, c] / samples)

    for d in range(1, loci):
        g, peer = any_peer(d)
        send(y.at[rows_of(g, blocks), :], ry.at[d], ry_s.at[0], ry_r.at[0], peer)
    score = y[own_rows, :]
    sent = y.at[pl.ds(0, (loci - 1) * blocks), :]
    landed = ry.at[pl.ds(1, loci - 1)]
    pltpu.make_async_copy(sent, sent, ry_s.at[0]).wait()
    pltpu.make_async_copy(landed, landed, ry_r.at[0]).wait()
    for d in range(1, loci):
        score = score + ry[d]
    for k in range(eff.shape[1] // BLK):
        hit = (block_row == first + k) & (block_row <= last)
        out_ref[:, k * BLK:(k + 1) * BLK] = jnp.sum(jnp.where(hit, score, 0.0), axis=0, keepdims=True)


def slab_body(dosages, reach_blk, locus_start, locus_end, locus_effects):
    n_var, n_smp, n_sub = (lax.axis_size(a) for a in ("var", "smp", "sub"))
    n_pl = n_smp * n_sub
    rows, stripe = dosages.shape
    blocks = reach_blk.shape[0]
    loci = locus_start.shape[0]
    f32 = jnp.float32
    dma = pltpu.SemaphoreType.DMA
    hbm = pl.BlockSpec(memory_space=pltpu.HBM)
    vmem = pl.BlockSpec(memory_space=pltpu.VMEM)
    return pl.pallas_call(
        functools.partial(kernel, n_var, n_smp, n_sub),
        out_shape=jax.ShapeDtypeStruct(locus_effects.shape, f32),
        in_specs=[hbm] * 5,
        out_specs=vmem,
        scratch_shapes=[
            pltpu.SMEM(reach_blk.shape, reach_blk.dtype),
            pltpu.SMEM(locus_start.shape, locus_start.dtype),
            pltpu.SMEM(locus_end.shape, locus_end.dtype),
            pltpu.VMEM(locus_effects.shape, locus_effects.dtype),
            pltpu.VMEM((rows, stripe), dosages.dtype),
            pltpu.VMEM((n_var, rows // n_var, stripe), dosages.dtype),
            pltpu.VMEM((n_pl, 2, stripe), f32),
            pltpu.VMEM((n_var, 2, stripe), f32),
            pltpu.VMEM((loci * blocks, BLK), f32),
            pltpu.VMEM((loci * blocks, BLK), f32),
            pltpu.VMEM((loci, blocks, BLK), f32),
            dma((4,)), dma((2,)),
            dma((n_var,)), dma((n_var,)),
            dma((n_pl,)), dma((n_pl,)),
            dma((n_var,)), dma((n_var,)),
            dma((n_var,)), dma((n_var,)),
            dma((n_pl,)), dma((n_pl,)),
            dma((1,)), dma((1,)),
        ],
        compiler_params=pltpu.CompilerParams(
            collective_id=0, has_side_effects=True, vmem_limit_bytes=60 * 1024 * 1024),
    )(dosages, reach_blk, locus_start, locus_end, locus_effects)


def body(dosages, reach_blk, locus_start, locus_end, locus_effects):
    blocks = reach_blk.shape[0]
    devices = lax.axis_size(("var", "smp", "sub"))
    short = blocks * BLK == locus_effects.shape[1] and locus_start.shape[0] == devices
    run = slab_body if short else wide_body
    return run(dosages, reach_blk, locus_start, locus_end, locus_effects)


def solution(mesh):
    in_specs = (
        P(("smp", "sub"), ("grp", "var")),
        P("grp"),
        P("grp"),
        P("grp"),
        P(("grp", "var", "smp", "sub"), None),
    )
    out_specs = P(("grp", "var", "smp", "sub"), None)
    return jax.shard_map(body, mesh=mesh, in_specs=in_specs, out_specs=out_specs, check_vma=False)
```

```python
import functools

import jax
import jax.numpy as jnp
from jax import lax
from jax.experimental import pallas as pl
from jax.experimental.pallas import tpu as pltpu
from jax.sharding import PartitionSpec as P

BLK = 128
REACH = 12
LMAX = 8


EPS = 1e-05
HIGHEST = lax.Precision.HIGHEST


def shifted(block, axis, distance):
    devices = range(lax.axis_size(axis))
    route = [(i - distance, i) for i in devices if i - distance in devices]
    return lax.ppermute(block, axis, route)


def slot_table(locus_start, locus_end, first_blk, window_blocks):
    lengths = locus_end - locus_start + 1
    slot_ids = jnp.arange(LMAX, dtype=jnp.int32)
    target = locus_start[:, None] + slot_ids[None, :] - first_blk
    live_slot = slot_ids[None, :] < lengths[:, None]
    blocks = jnp.arange(window_blocks, dtype=jnp.int32)
    hits = live_slot[:, :, None] & (target[:, :, None] == blocks[None, None, :])
    return jnp.where(hits, 1.0, 0.0).astype(jnp.float32)


def fetch_ahead(dosages, halo_cols):
    stripe = dosages.shape[1]
    hops = (halo_cols + stripe - 1) // stripe
    pieces = [dosages]
    for distance in range(1, hops + 1):
        pieces.append(shifted(dosages, "var", -distance))
    joined = jnp.concatenate(pieces, axis=1)
    return joined


def wide_body(dosages, reach_blk, locus_start, locus_end, locus_effects):
    row_local, stripe = dosages.shape
    block_count = reach_blk.shape[0]
    locus_count = locus_start.shape[0]
    halo_cols = REACH * BLK
    window = fetch_ahead(dosages, halo_cols)
    win_cols = window.shape[1]
    shards = lax.axis_size(("smp", "sub"))
    samples = row_local * shards
    col_sum = lax.psum(jnp.sum(window, axis=0, dtype=jnp.float32), ("smp", "sub"))
    col_mean = col_sum / samples
    centred = jnp.sum(jnp.square(window.astype(jnp.float32) - col_mean[None, :]), axis=0)
    spread = lax.psum(centred, ("smp", "sub"))
    inv_sd = lax.rsqrt(spread / samples + EPS)
    cross_prod = lax.dot_general(
        dosages, window, (((0,), (0,)), ((), ())), preferred_element_type=jnp.float32
    )
    row_first = jnp.int32(0)
    ld_corr = (cross_prod / samples - col_mean[:stripe, None] * col_mean[None, :] / shards) * (
        inv_sd[:stripe, None] * inv_sd[None, :]
    )
    stripe_blocks = stripe // BLK
    first_blk = lax.axis_index("var") * stripe_blocks
    reach_local = lax.dynamic_slice_in_dim(reach_blk, first_blk, stripe_blocks)
    row_blocks = jnp.arange(stripe, dtype=jnp.int32) // BLK
    stripe_ids = jnp.arange(stripe_blocks, dtype=jnp.int32)
    reach_rows = jnp.sum(
        jnp.where(row_blocks[:, None] == stripe_ids[None, :], reach_local[None, :], 0), axis=1
    )
    col_blocks = jnp.arange(win_cols, dtype=jnp.int32) // BLK
    block_gap = col_blocks[None, :] - row_blocks[:, None]
    keep_mask = (
        (block_gap >= 0)
        & (block_gap <= reach_rows[:, None])
        & (first_blk + col_blocks[None, :] < block_count)
    )
    band_corr = jnp.where(keep_mask, ld_corr, 0.0)
    strict = jnp.where(block_gap > 0, band_corr, 0.0)
    window_blocks = win_cols // BLK
    lookup = slot_table(locus_start, locus_end, first_blk, window_blocks)
    gathered = lax.all_gather(locus_effects, ("var", "smp", "sub"), axis=0, tiled=True)
    effects = gathered.astype(jnp.float32).reshape(locus_count, LMAX, BLK)
    b_window = jnp.einsum("lkw,lkc->lwc", lookup, effects, precision=HIGHEST).reshape(
        locus_count, win_cols
    )
    b_rows = lax.dynamic_slice_in_dim(b_window, row_first, stripe, 1)
    y_rows = jnp.dot(b_window, band_corr.T, precision=HIGHEST)
    y_cols = jnp.dot(b_rows, strict, precision=HIGHEST)
    y_window = y_cols + lax.dynamic_update_slice_in_dim(
        jnp.zeros_like(y_cols), y_rows, row_first, 1
    )
    scores = jnp.einsum(
        "lkw,lwc->lkc", lookup, y_window.reshape(locus_count, window_blocks, BLK), precision=HIGHEST
    )
    return lax.psum_scatter(
        scores.reshape(locus_count, LMAX * BLK),
        ("var", "smp", "sub"),
        scatter_dimension=0,
        tiled=True,
    )


MESH = pl.DeviceIdType.MESH


def halves(values):
    high = values.astype(jnp.bfloat16)
    low = (values - high.astype(jnp.float32)).astype(jnp.bfloat16)
    return jnp.concatenate([high, low], axis=0)


def rejoined(pair):
    half = pair.shape[0] // 2
    return pair[:half].astype(jnp.float32) + pair[half:].astype(jnp.float32)


def kernel(n_var, n_smp, n_sub, dos_any, reach_any, start_any, end_any, eff_any, out_ref,
           reach, start, end, eff_ref, local, x, st, ms, e, y, ry,
           small_sem, local_sem, x_s, x_r, st_s, st_r, ms_s, ms_r, e1_s, e1_r, e2_s, e2_r,
           ry_s, ry_r):
    n_pl = n_smp * n_sub
    rows, stripe = dos_any.shape
    part = rows // n_var
    per_stripe = stripe // BLK
    blocks = n_var * per_stripe
    loci = n_var * n_pl
    samples = rows * n_pl
    v = lax.axis_index("var")
    p = lax.axis_index("smp") * n_sub + lax.axis_index("sub")

    def var_peer(d):
        t = lax.rem(v + d, n_var)
        return t, {"var": t}

    def plane_peer(d):
        q = lax.rem(p + d, n_pl)
        return q, {"smp": lax.div(q, n_sub), "sub": lax.rem(q, n_sub)}

    def any_peer(d):
        g = lax.rem(p * n_var + v + d, loci)
        q = lax.div(g, n_var)
        return g, {"var": lax.rem(g, n_var), "smp": lax.div(q, n_sub), "sub": lax.rem(q, n_sub)}

    def rows_of(index, count):
        return pl.ds(pl.multiple_of(index * count, count), count)

    def send(src, dst, s_sem, r_sem, peer):
        copy = pltpu.make_async_remote_copy(
            src_ref=src, dst_ref=dst, send_sem=s_sem, recv_sem=r_sem,
            device_id=peer, device_id_type=MESH)
        copy.start()
        return copy

    barrier = pltpu.get_barrier_semaphore()
    for d in range(1, loci):
        pl.semaphore_signal(barrier, inc=1, device_id=any_peer(d)[1], device_id_type=MESH)

    small = [pltpu.make_async_copy(src, dst, small_sem.at[n]) for n, (src, dst) in enumerate((
        (eff_any, eff_ref), (start_any, start), (end_any, end), (reach_any, reach)))]
    for copy in small:
        copy.start()
    whole = pltpu.make_async_copy(dos_any, local, local_sem.at[0])
    whole.start()
    own = pltpu.make_async_copy(dos_any.at[rows_of(v, part), :], x.at[v], local_sem.at[1])
    own.start()

    for copy in small:
        copy.wait()
    me = v * n_pl + p
    first, last = start[me], end[me]
    block_row = lax.broadcasted_iota(jnp.int32, (blocks, BLK), 0)
    eff = eff_ref[...].astype(jnp.float32)
    placed = jnp.zeros((blocks, BLK), jnp.float32)
    for k in range(eff.shape[1] // BLK):
        hit = (block_row == first + k) & (block_row <= last)
        placed = placed + jnp.where(hit, eff[:, k * BLK:(k + 1) * BLK], 0.0)
    own_rows = rows_of(p * n_var + v, blocks)
    e[own_rows, :] = placed

    whole.wait()
    mine = local[...].astype(jnp.float32)
    total = jnp.sum(mine, axis=0, keepdims=True)
    sq = jnp.sum(jnp.square(mine - total / rows), axis=0, keepdims=True)
    st[p, 0:1, :] = total
    st[p, 1:2, :] = sq
    pl.semaphore_wait(barrier, loci - 1)
    e1 = [send(e.at[own_rows, :], e.at[own_rows, :], e1_s.at[d], e1_r.at[d], var_peer(d)[1])
          for d in range(1, n_var)]
    sts = [send(st.at[p], st.at[p], st_s.at[d], st_r.at[d], plane_peer(d)[1])
           for d in range(1, n_pl)]
    xs = []
    for d in range(1, n_var):
        t, peer = var_peer(d)
        xs.append(send(dos_any.at[rows_of(t, part), :], x.at[v], x_s.at[d], x_r.at[d], peer))

    for copy in e1:
        copy.wait()
    group = rows_of(p, n_var * blocks)
    e2 = [send(e.at[group, :], e.at[group, :], e2_s.at[d], e2_r.at[d], plane_peer(d)[1])
          for d in range(1, n_pl)]

    for copy in sts:
        copy.wait()
    mean = st[0, 0:1, :]
    for q in range(1, n_pl):
        mean = mean + st[q, 0:1, :]
    mean = mean / samples
    spread = jnp.zeros_like(mean)
    for q in range(n_pl):
        spread = spread + (st[q, 1:2, :] + rows * jnp.square(st[q, 0:1, :] / rows - mean))
    ms[v, 0:1, :] = mean
    var_eps = spread / samples + EPS
    inv = lax.rsqrt(var_eps)
    ms[v, 1:2, :] = inv * (1.5 - 0.5 * var_eps * inv * inv)
    mss = [send(ms.at[v], ms.at[v], ms_s.at[d], ms_r.at[d], var_peer(d)[1])
           for d in range(1, n_var)]
    for copy in e2:
        copy.wait()
    for copy in mss:
        copy.wait()
    own.wait()
    for copy in xs:
        copy.wait()

    def cols(j):
        return j // per_stripe, slice((j % per_stripe) * BLK, (j % per_stripe + 1) * BLK)

    parts = []
    for j in range(blocks):
        s, c = cols(j)
        z = e[pl.ds(j, loci, stride=blocks), :] * ms[s, 1:2, c]
        pair = halves(z)
        w = lax.dot_general(pair, x[s, :, c], (((1,), (1,)), ((), ())),
                            preferred_element_type=jnp.float32)
        shift = jnp.sum(rejoined(pair) * ms[s, 0:1, c], axis=1, keepdims=True)
        parts.append(w[:loci] + w[loci:] - shift)
    bands = []
    for i in range(blocks):
        summed = parts[i]
        for j in range(blocks):
            if j != i:
                low, high = min(i, j), max(i, j)
                summed = summed + jnp.where(reach[low] >= high - low, 1.0, 0.0) * parts[j]
        bands.append(summed)
    half = loci // 2
    here = p * n_var + v
    for group_of in range(2):
        base = group_of * half
        for i in range(blocks):
            s, c = cols(i)
            r = lax.dot_general(halves(bands[i][base:base + half]), x[s, :, c],
                                (((1,), (0,)), ((), ())), preferred_element_type=jnp.float32)
            y[pl.ds(base * blocks + i, half, stride=blocks), :] = (
                r[:half] + r[half:]) * (ms[s, 1:2, c] / samples)
        for g in range(base, base + half):
            q = g // n_var
            peer = {"var": g % n_var, "smp": q // n_sub, "sub": q % n_sub}

            @pl.when(here != g)
            def _():
                send(y.at[pl.ds(g * blocks, blocks), :], ry.at[lax.rem(g - here + loci, loci)],
                     ry_s.at[0], ry_r.at[0], peer)
    score = y[own_rows, :]
    sent = y.at[pl.ds(0, (loci - 1) * blocks), :]
    landed = ry.at[pl.ds(1, loci - 1)]
    pltpu.make_async_copy(sent, sent, ry_s.at[0]).wait()
    pltpu.make_async_copy(landed, landed, ry_r.at[0]).wait()
    for d in range(1, loci):
        score = score + ry[d]
    for k in range(eff.shape[1] // BLK):
        hit = (block_row == first + k) & (block_row <= last)
        out_ref[:, k * BLK:(k + 1) * BLK] = jnp.sum(jnp.where(hit, score, 0.0), axis=0, keepdims=True)


def slab_body(dosages, reach_blk, locus_start, locus_end, locus_effects):
    n_var, n_smp, n_sub = (lax.axis_size(a) for a in ("var", "smp", "sub"))
    n_pl = n_smp * n_sub
    rows, stripe = dosages.shape
    blocks = reach_blk.shape[0]
    loci = locus_start.shape[0]
    f32 = jnp.float32
    dma = pltpu.SemaphoreType.DMA
    hbm = pl.BlockSpec(memory_space=pltpu.HBM)
    vmem = pl.BlockSpec(memory_space=pltpu.VMEM)
    return pl.pallas_call(
        functools.partial(kernel, n_var, n_smp, n_sub),
        out_shape=jax.ShapeDtypeStruct(locus_effects.shape, f32),
        in_specs=[hbm] * 5,
        out_specs=vmem,
        scratch_shapes=[
            pltpu.SMEM(reach_blk.shape, reach_blk.dtype),
            pltpu.SMEM(locus_start.shape, locus_start.dtype),
            pltpu.SMEM(locus_end.shape, locus_end.dtype),
            pltpu.VMEM(locus_effects.shape, locus_effects.dtype),
            pltpu.VMEM((rows, stripe), dosages.dtype),
            pltpu.VMEM((n_var, rows // n_var, stripe), dosages.dtype),
            pltpu.VMEM((n_pl, 2, stripe), f32),
            pltpu.VMEM((n_var, 2, stripe), f32),
            pltpu.VMEM((loci * blocks, BLK), f32),
            pltpu.VMEM((loci * blocks, BLK), f32),
            pltpu.VMEM((loci, blocks, BLK), f32),
            dma((4,)), dma((2,)),
            dma((n_var,)), dma((n_var,)),
            dma((n_pl,)), dma((n_pl,)),
            dma((n_var,)), dma((n_var,)),
            dma((n_var,)), dma((n_var,)),
            dma((n_pl,)), dma((n_pl,)),
            dma((1,)), dma((1,)),
        ],
        compiler_params=pltpu.CompilerParams(
            collective_id=0, has_side_effects=True, vmem_limit_bytes=60 * 1024 * 1024),
    )(dosages, reach_blk, locus_start, locus_end, locus_effects)


def body(dosages, reach_blk, locus_start, locus_end, locus_effects):
    blocks = reach_blk.shape[0]
    devices = lax.axis_size(("var", "smp", "sub"))
    short = blocks * BLK == locus_effects.shape[1] and locus_start.shape[0] == devices
    run = slab_body if short else wide_body
    return run(dosages, reach_blk, locus_start, locus_end, locus_effects)


def solution(mesh):
    in_specs = (
        P(("smp", "sub"), ("grp", "var")),
        P("grp"),
        P("grp"),
        P("grp"),
        P(("grp", "var", "smp", "sub"), None),
    )
    out_specs = P(("grp", "var", "smp", "sub"), None)
    return jax.shard_map(body, mesh=mesh, in_specs=in_specs, out_specs=out_specs, check_vma=False)
```
